32 devices in a mesh: row: 8 (over z, x), col: 4 (over y, core).
Axes of the slice: x: 2, y: 2, z: 4, core: 2. Of those that a mesh axis runs over, the one named last changes fastest.
Arguments:
- activations: bfloat16 [8, 1024, 8192], P(None, 'col', 'row'), may hold values from -6 to 6
- output_gradients: bfloat16 [8, 1024, 8192], P(None, 'row', 'col'), may hold values from -6 to 6
- second_moment: float32 [8192, 8192], P('col', 'row'), may hold values from 0.0001 to 1, as said below
- proj_out: bfloat16 [256, 8192], P(None, 'col'), may hold values from -0.13258252 to 0.13258252
- proj_in: bfloat16 [256, 8192], P(None, 'row'), may hold values from -0.0625 to 0.0625
- queries: bfloat16 [2048, 65536], P(None, ('row', 'col')), may hold values from -6 to 6
Outputs:
- scores: float32 [8, 2048], replicated
The draws below stay inside these ranges and needn't reach their ends.
Inputs may be any that keep to these rules, and one draw needn't show every extreme that they name: second_moment is positive.
All inputs are finite; a program needn't handle non-finite values.
Results may differ from the reference program's by a relative error of at most 0.0003.
Values may be sent and summed in bfloat16 or wider, within the bound.
A program may use at most 256 MiB of HBM per device.

```python
import jax
import jax.numpy as jnp
from jax import lax

D_IN = 8192
D_OUT = 8192
K_IN = 256
K_OUT = 256
SEQ = 1024
SCORED_EXAMPLES = 8
NQ = 2048


def draw_second_moment(key, part):
    logs = jax.random.uniform(key, (D_OUT, D_IN), jnp.float32, -4.6, 0.0)
    column = jnp.arange(D_IN, dtype=jnp.float32) / D_IN
    values = jnp.exp(logs) / (1.0 + 8.0 * column)[None, :]
    return jnp.maximum(values, 0.0001).astype(jnp.float32)


def draw_proj_out(key, part):
    rank = jnp.arange(K_OUT, dtype=jnp.float32) / K_OUT
    base = jnp.clip(jax.random.normal(key, (K_OUT, D_OUT), jnp.float32), -4.0, 4.0)
    rising = 1.0 + 2.0 * rank
    values = base * rising[:, None] * float(D_OUT) ** (-0.5)
    return values.astype(jnp.bfloat16)


def block_scale(rng, shape, split, smallest, top_value):
    loudness = 1.0
    for dim, parts in split:
        steps = jax.random.uniform(jax.random.fold_in(jax.random.fold_in(rng, 6), dim), (parts,), jnp.float32, smallest / len(split), top_value / len(split))
        loudness = loudness * jnp.repeat(jnp.exp(steps), shape[dim] // parts).reshape((-1,) + (1,) * (len(shape) - 1 - dim))
    return loudness


def normal_values(rng, extent, width, most, split=(), held_as=jnp.bfloat16):
    result = width * jax.random.normal(rng, extent, jnp.float32)
    if split:
        result = result * block_scale(rng, extent, split, -0.22, 0.18)
    return jnp.clip(result, -most, most).astype(held_as)


def setup_inputs(seed: int = 0) -> dict:
    splits = jax.random.split(jax.random.key(seed), 7)
    return {
        "activations": normal_values(splits[0], (SCORED_EXAMPLES, SEQ, D_IN), 1.0, 6.0, ((1, 4), (2, 8))),
        "output_gradients": normal_values(splits[1], (SCORED_EXAMPLES, SEQ, D_OUT), 1.0, 6.0, ((1, 8), (2, 4))),
        "second_moment": draw_second_moment(jax.random.fold_in(splits[6], 71), 0),
        "proj_out": draw_proj_out(jax.random.fold_in(splits[6], 71), 0),
        "proj_in": normal_values(splits[4], (K_IN, D_IN), D_IN ** -0.5, 0.0625, ((1, 8),)),
        "queries": normal_values(splits[5], (NQ, K_OUT * K_IN), 1.0, 6.0, ((1, 32),)),
    }


def reference(activations, output_gradients, second_moment, proj_out, proj_in, queries):
    scale = lax.rsqrt(second_moment + 1e-08)
    pout_f = proj_out.astype(jnp.float32)
    pin_f = proj_in.astype(jnp.float32)

    def one_example(pair):
        acts, grads = pair
        tile = jnp.dot(grads.T, acts, preferred_element_type=jnp.float32)
        corrected = tile * scale
        partial_amount = jnp.dot(pout_f, corrected, precision=lax.Precision.HIGHEST)
        projected = jnp.dot(partial_amount, pin_f.T, precision=lax.Precision.HIGHEST)
        return projected.reshape(K_OUT * K_IN)
    projected = lax.map(one_example, (activations, output_gradients))
    sq = lax.optimization_barrier(jnp.sum(projected * projected, axis=1))
    raw = jnp.dot(projected, queries.astype(jnp.float32).T, precision=lax.Precision.HIGHEST)
    return raw * lax.rsqrt(sq + 1e-06)[:, None]
```

```python
import functools

import jax
import jax.numpy as jnp
from jax import lax
from jax.experimental import pallas as pl
from jax.experimental.pallas import tpu as pltpu
from jax.sharding import PartitionSpec as P

MESH = pl.DeviceIdType.MESH
F32 = jnp.float32
BF16 = jnp.bfloat16


def split2(v):
    hi = v.astype(BF16)
    return hi, (v - hi.astype(F32)).astype(BF16)


def kernel(nrow, ncol, nz, act, grad, smom, pout, pin, qry, out, gall, aall,
           gbuf, abuf, scale, qbuf, part, loc, rs, red, sc_src, sc_buf, fin,
           lsem, ldsem, grecv, upsem, dnsem, xsem, arecv, asem,
           rs_send, rs_recv, sc_send, sc_recv, fin_send, fin_recv):
    nx = nrow // nz
    nd = nrow * ncol
    ne, tr, nc = grad.shape
    tc, ni = act.shape[1], act.shape[2]
    ko, ki = pout.shape[0], pin.shape[0]
    own_rows = ko // nd
    pieces = fin.shape[0]
    stride = nd // pieces
    r = lax.axis_index("row")
    c = lax.axis_index("col")
    z, x = r // nx, r % nx
    me = r * ncol + c

    def spot(d):
        return {"row": d // ncol, "col": d % ncol}

    barrier = pltpu.get_barrier_semaphore()

    def greet(k, carry):
        pl.semaphore_signal(barrier, inc=1, device_id=spot((me + k) % nd), device_id_type=MESH)
        return carry

    local = [
        pltpu.make_async_copy(smom, scale, lsem.at[0]),
        pltpu.make_async_copy(qry, qbuf, lsem.at[1]),
        pltpu.make_async_copy(grad, gall.at[:, pl.ds(r * tr, tr), :], lsem.at[2]),
        pltpu.make_async_copy(act, aall.at[:, pl.ds(c * tc, tc), :], lsem.at[3]),
    ]
    lax.fori_loop(1, nd, greet, 0)
    for copy in local:
        copy.start()
    pl.semaphore_wait(barrier, nd - 1)

    def block(e, row):
        return gall.at[e, pl.ds(row * tr, tr), :]

    def g_copy(e, zs, send_sem, target, own=False):
        row = zs * nx + x
        return pltpu.make_async_remote_copy(
            src_ref=grad.at[e] if own else block(e, row),
            dst_ref=block(e, row),
            send_sem=send_sem,
            recv_sem=grecv.at[e, row],
            device_id={"row": target},
            device_id_type=MESH,
        )

    def up(e, zs, own=False):
        return g_copy(e, zs, upsem.at[e, zs], (z + 1) * nx + x, own)

    def down(e, zs, own=False):
        return g_copy(e, zs, dnsem.at[e, zs], (z - 1) * nx + x, own)

    def across(e, zs, k, own=False):
        return g_copy(e, zs, xsem.at[e, zs, k], z * nx + (x + k) % nx, own)

    def a_copy(e, k):
        rows = pl.ds(c * tc, tc)
        return pltpu.make_async_remote_copy(
            src_ref=act.at[e],
            dst_ref=aall.at[e, rows, :],
            send_sem=asem.at[e, k],
            recv_sem=arecv.at[e, c],
            device_id={"col": (c + k) % ncol},
            device_id_type=MESH,
        )

    def g_arrived(e, row):
        pltpu.make_async_copy(block(e, row), block(e, row), grecv.at[e, row]).wait()

    def own_sends(e):
        @pl.when(z < nz - 1)
        def _():
            up(e, z, True).start()

        @pl.when(z > 0)
        def _():
            down(e, z, True).start()

        for k in range(1, nx):
            across(e, z, k, True).start()
        for k in range(1, ncol):
            a_copy(e, k).start()

    def forward(e, d):
        @pl.when(z - d >= 0)
        def _():
            zs = z - d
            g_arrived(e, zs * nx + x)

            @pl.when(z < nz - 1)
            def _():
                up(e, zs).start()

            for k in range(1, nx):
                across(e, zs, k).start()

        @pl.when(z + d < nz)
        def _():
            zs = z + d
            g_arrived(e, zs * nx + x)

            @pl.when(z > 0)
            def _():
                down(e, zs).start()

            for k in range(1, nx):
                across(e, zs, k).start()

    def loads(e):
        return (
            pltpu.make_async_copy(gall.at[e], gbuf, ldsem.at[0]),
            pltpu.make_async_copy(aall.at[e], abuf, ldsem.at[1]),
        )

    def load(e):
        for k in range(1, nx):
            for zs in range(nz):
                g_arrived(e, zs * nx + (x + k) % nx)
        for k in range(1, ncol):
            rows = pl.ds(((c + k) % ncol) * tc, tc)
            whole = aall.at[e, rows, :]
            pltpu.make_async_copy(whole, whole, arecv.at[e, (c + k) % ncol]).wait()
        for copy in loads(e):
            copy.start()

    def rs_block(d):
        return pl.ds(pl.multiple_of((d * own_rows) // 8 * 8, 8), 8)

    width = min(512, nc)

    def compute(e):
        for copy in loads(e):
            copy.wait()
        part[...] = jnp.zeros_like(part)

        def columns(j, carry):
            cols = pl.ds(pl.multiple_of(j * width, width), width)
            tile = lax.dot_general(
                gbuf[:, cols], abuf[...], (((0,), (0,)), ((), ())), preferred_element_type=F32
            )
            hi, lo = split2(tile * scale[cols, :])
            po = pout[:, cols]
            part[...] += jnp.dot(po, hi, preferred_element_type=F32) + jnp.dot(
                po, lo, preferred_element_type=F32
            )
            return carry

        lax.fori_loop(0, nc // width, columns, 0)
        hi, lo = split2(part[...])
        nt = (((1,), (1,)), ((), ()))
        loc[e] = lax.dot_general(hi, pin[...], nt, preferred_element_type=F32) + lax.dot_general(
            lo, pin[...], nt, preferred_element_type=F32
        )
        rs[me, e] = loc[e, rs_block(me), :]

        def send(k, carry):
            d = (me + k) % nd
            pltpu.make_async_remote_copy(
                src_ref=loc.at[e, rs_block(d), :],
                dst_ref=rs.at[me, e],
                send_sem=rs_send,
                recv_sem=rs_recv,
                device_id=spot(d),
                device_id_type=MESH,
            ).start()
            return carry

        lax.fori_loop(1, nd, send, 0)

    own_sends(0)
    own_sends(1)
    local[0].wait()
    lines = min(256, nc)

    def invert(j, carry):
        rows = pl.ds(pl.multiple_of(j * lines, lines), lines)
        scale[rows, :] = lax.rsqrt(scale[rows, :] + 1e-08)
        return carry

    lax.fori_loop(0, nc // lines, invert, 0)
    for copy in local[1:]:
        copy.wait()

    def step(s, carry):
        @pl.when(s + 2 < ne)
        def _():
            own_sends(s + 2)

        for d in range(1, nz):
            @pl.when((s - d + 1 >= 0) & (s - d + 1 < ne))
            def _():
                forward(s - d + 1, d)

        @pl.when(s - nz >= 0)
        def _():
            compute(s - nz)

        @pl.when((s - nz + 1 >= 0) & (s - nz + 1 < ne))
        def _():
            load(s - nz + 1)

        return carry

    lax.fori_loop(0, ne + nz, step, 0)

    def sent(e, carry):
        for k in range(1, ncol):
            a_copy(e, k).wait_send()
        for zs in range(nz):
            for k in range(1, nx):
                across(e, zs, k).wait_send()

            @pl.when((zs <= z) & (z < nz - 1))
            def _():
                up(e, zs).wait_send()

            @pl.when((zs >= z) & (z > 0))
            def _():
                down(e, zs).wait_send()

        return carry

    landed = rs.at[pl.ds(0, nd - 1)]
    pltpu.make_async_copy(landed, landed, rs_recv).wait()
    red[...] = lax.fori_loop(1, nd, lambda k, v: v + rs[k], rs[0])
    first = (me * own_rows) % 8 if own_rows < 8 else 0
    squares = jnp.zeros((ne, ki), F32)
    total = jnp.zeros((3 * ne, qbuf.shape[0]), F32)
    for k in range(own_rows):
        row = red[:, first + k, :]
        squares += row * row
        hi = row.astype(BF16).astype(F32)
        mid = (row - hi).astype(BF16).astype(F32)
        lhs = jnp.concatenate([hi, mid, row - hi - mid], axis=0).astype(BF16)
        total += lax.dot_general(
            lhs, qbuf[:, k * ki:(k + 1) * ki], (((1,), (1,)), ((), ())), preferred_element_type=F32
        )
    scores = total[:ne] + total[ne:2 * ne] + total[2 * ne:]
    sq = jnp.broadcast_to(jnp.sum(squares, axis=1, keepdims=True), (ne, 128))
    for p in range(pieces):
        sc_src[p, 0] = scores[:, p * 128:(p + 1) * 128]
        sc_src[p, 1] = sq

    mine = me // stride
    reducer = me % stride == 0

    def to_reducer(p, carry):
        @pl.when(p * stride != me)
        def _():
            pltpu.make_async_remote_copy(
                src_ref=sc_src.at[p],
                dst_ref=sc_buf.at[me],
                send_sem=sc_send,
                recv_sem=sc_recv,
                device_id=spot(p * stride),
                device_id_type=MESH,
            ).start()

        return carry

    lax.fori_loop(0, pieces, to_reducer, 0)

    @pl.when(reducer)
    def _():
        sc_buf[me] = sc_src[mine]
        whole = sc_buf.at[pl.ds(0, nd - 1)]
        pltpu.make_async_copy(whole, whole, sc_recv).wait()
        both = lax.fori_loop(1, nd, lambda k, v: v + sc_buf[k], sc_buf[0])
        fin[mine] = both[0] * lax.rsqrt(both[1] + 1e-06)

        def to_all(k, carry):
            pltpu.make_async_remote_copy(
                src_ref=fin.at[mine],
                dst_ref=fin.at[mine],
                send_sem=fin_send,
                recv_sem=fin_recv,
                device_id=spot((me + k) % nd),
                device_id_type=MESH,
            ).start()
            return carry

        lax.fori_loop(1, nd, to_all, 0)

    lax.fori_loop(0, ne, sent, 0)
    pltpu.make_async_copy(landed, landed, rs_send).wait()

    def finish(count):
        src = sc_src.at[pl.ds(0, count)]
        pltpu.make_async_copy(src, src, sc_send).wait()
        got = fin.at[pl.ds(0, count)]
        pltpu.make_async_copy(got, got, fin_recv).wait()

    @pl.when(reducer)
    def _():
        finish(pieces - 1)
        gone = sc_buf.at[pl.ds(0, nd - 1), 0]
        pltpu.make_async_copy(gone, gone, fin_send).wait()

    @pl.when(jnp.logical_not(reducer))
    def _():
        finish(pieces)

    for p in range(pieces):
        out[:, p * 128:(p + 1) * 128] = fin[p]


def body(nrow, ncol, activations, output_gradients, second_moment, proj_out, proj_in, queries):
    ne, tc, ni = activations.shape
    tr, nc = output_gradients.shape[1:]
    ko, ki = proj_out.shape[0], proj_in.shape[0]
    nq, nf = queries.shape
    nz = 4 if nrow % 4 == 0 else 1
    nd = nrow * ncol
    pieces = nq // 128
    while nd % pieces:
        pieces //= 2
    seq = tr * nrow
    dma = pltpu.SemaphoreType.DMA
    hbm = pl.BlockSpec(memory_space=pl.ANY)
    vmem = pl.BlockSpec(memory_space=pltpu.VMEM)
    return pl.pallas_call(
        functools.partial(kernel, nrow, ncol, nz),
        out_shape=(
            jax.ShapeDtypeStruct((ne, nq), F32),
            jax.ShapeDtypeStruct((ne, seq, nc), BF16),
            jax.ShapeDtypeStruct((ne, seq, ni), BF16),
        ),
        in_specs=[hbm, hbm, hbm, vmem, vmem, hbm],
        out_specs=(vmem, hbm, hbm),
        scratch_shapes=[
            pltpu.VMEM((seq, nc), BF16),
            pltpu.VMEM((seq, ni), BF16),
            pltpu.VMEM((nc, ni), F32),
            pltpu.VMEM((nq, nf), BF16),
            pltpu.VMEM((ko, ni), F32),
            pltpu.VMEM((ne, ko, ki), F32),
            pltpu.VMEM((nd, ne, 8, ki), F32),
            pltpu.VMEM((ne, 8, ki), F32),
            pltpu.VMEM((pieces, 2, ne, 128), F32),
            pltpu.VMEM((nd, 2, ne, 128), F32),
            pltpu.VMEM((pieces, ne, 128), F32),
            dma((4,)),
            dma((2,)),
            dma((ne, nrow)),
            dma((ne, nz)),
            dma((ne, nz)),
            dma((ne, nz, nrow // nz)),
            dma((ne, ncol)),
            dma((ne, ncol)),
            dma, dma, dma, dma, dma, dma,
        ],
        compiler_params=pltpu.CompilerParams(
            collective_id=0, has_side_effects=True, vmem_limit_bytes=58 * 2**20
        ),
    )(activations, output_gradients, second_moment, proj_out, proj_in, queries)[0]


def solution(mesh):
    in_specs = (
        P(None, "col", "row"),
        P(None, "row", "col"),
        P("col", "row"),
        P(None, "col"),
        P(None, "row"),
        P(None, ("row", "col")),
    )
    run = functools.partial(body, mesh.shape["row"], mesh.shape["col"])
    return jax.shard_map(run, mesh=mesh, in_specs=in_specs, out_specs=P(), check_vma=False)
```

```python
import functools

import jax
import jax.numpy as jnp
from jax import lax
from jax.experimental import pallas as pl
from jax.experimental.pallas import tpu as pltpu
from jax.sharding import PartitionSpec as P

MESH = pl.DeviceIdType.MESH
F32 = jnp.float32
BF16 = jnp.bfloat16


def split2(v):
    hi = v.astype(BF16)
    return hi, (v - hi.astype(F32)).astype(BF16)


def kernel(nrow, ncol, nz, act, grad, smom, pout, pin, qry, out, gall, aall,
           gbuf, abuf, scale, qbuf, part, loc, rs, red, sc_src, sc_buf, fin,
           lsem, ldsem, grecv, upsem, dnsem, xsem, arecv, asem,
           rs_send, rs_recv, sc_send, sc_recv, fin_send, fin_recv):
    nx = nrow // nz
    nd = nrow * ncol
    ne, tr, nc = grad.shape
    tc, ni = act.shape[1], act.shape[2]
    ko, ki = pout.shape[0], pin.shape[0]
    own_rows = ko // nd
    pieces = fin.shape[0]
    stride = nd // pieces
    r = lax.axis_index("row")
    c = lax.axis_index("col")
    z, x = r // nx, r % nx
    me = r * ncol + c

    def spot(d):
        return {"row": d // ncol, "col": d % ncol}

    barrier = pltpu.get_barrier_semaphore()

    def greet(k, carry):
        pl.semaphore_signal(barrier, inc=1, device_id=spot((me + k) % nd), device_id_type=MESH)
        return carry

    local = [
        pltpu.make_async_copy(smom, scale, lsem.at[0]),
        pltpu.make_async_copy(qry, qbuf, lsem.at[1]),
    ]
    lax.fori_loop(1, nd, greet, 0)
    for copy in local:
        copy.start()
    pl.semaphore_wait(barrier, nd - 1)

    def block(e, row):
        return gall.at[e, pl.ds(row * tr, tr), :]

    def g_copy(e, zs, send_sem, target, own=False):
        row = zs * nx + x
        return pltpu.make_async_remote_copy(
            src_ref=grad.at[e] if own else block(e, row),
            dst_ref=block(e, row),
            send_sem=send_sem,
            recv_sem=grecv.at[e, row],
            device_id={"row": target},
            device_id_type=MESH,
        )

    def up(e, zs, own=False):
        return g_copy(e, zs, upsem.at[e, zs], (z + 1) * nx + x, own)

    def down(e, zs, own=False):
        return g_copy(e, zs, dnsem.at[e, zs], (z - 1) * nx + x, own)

    def across(e, zs, k, own=False):
        return g_copy(e, zs, xsem.at[e, zs, k], z * nx + (x + k) % nx, own)

    def a_copy(e, k):
        rows = pl.ds(c * tc, tc)
        return pltpu.make_async_remote_copy(
            src_ref=act.at[e],
            dst_ref=aall.at[e, rows, :],
            send_sem=asem.at[e, k],
            recv_sem=arecv.at[e, c],
            device_id={"col": (c + k) % ncol},
            device_id_type=MESH,
        )

    def g_arrived(e, row):
        pltpu.make_async_copy(block(e, row), block(e, row), grecv.at[e, row]).wait()

    def own_sends(e):
        @pl.when(z < nz - 1)
        def _():
            up(e, z, True).start()

        @pl.when(z > 0)
        def _():
            down(e, z, True).start()

        for k in range(1, nx):
            across(e, z, k, True).start()
        for k in range(1, ncol):
            a_copy(e, k).start()

    def forward(e, d):
        @pl.when(z - d >= 0)
        def _():
            zs = z - d
            g_arrived(e, zs * nx + x)

            @pl.when(z < nz - 1)
            def _():
                up(e, zs).start()

            for k in range(1, nx):
                across(e, zs, k).start()

        @pl.when(z + d < nz)
        def _():
            zs = z + d
            g_arrived(e, zs * nx + x)

            @pl.when(z > 0)
            def _():
                down(e, zs).start()

            for k in range(1, nx):
                across(e, zs, k).start()

    def loads(e):
        copies = []
        for k in range(nrow):
            rows = pl.ds(((r + k) % nrow) * tr, tr)
            src = gall.at[e, rows, :] if k else grad.at[e]
            copies.append(pltpu.make_async_copy(src, gbuf.at[rows, :], ldsem.at[k]))
        for k in range(ncol):
            rows = pl.ds(((c + k) % ncol) * tc, tc)
            src = aall.at[e, rows, :] if k else act.at[e]
            copies.append(pltpu.make_async_copy(src, abuf.at[rows, :], ldsem.at[nrow + k]))
        return copies

    def load(e):
        for k in range(1, nx):
            for zs in range(nz):
                g_arrived(e, zs * nx + (x + k) % nx)
        for k in range(1, ncol):
            rows = pl.ds(((c + k) % ncol) * tc, tc)
            whole = aall.at[e, rows, :]
            pltpu.make_async_copy(whole, whole, arecv.at[e, (c + k) % ncol]).wait()
        for copy in loads(e):
            copy.start()

    def rs_block(d):
        return pl.ds(pl.multiple_of((d * own_rows) // 8 * 8, 8), 8)

    width = min(512, nc)

    def compute(e):
        for copy in loads(e):
            copy.wait()
        part[...] = jnp.zeros_like(part)

        def columns(j, carry):
            cols = pl.ds(pl.multiple_of(j * width, width), width)
            tile = lax.dot_general(
                gbuf[:, cols], abuf[...], (((0,), (0,)), ((), ())), preferred_element_type=F32
            )
            hi, lo = split2(tile * scale[cols, :])
            po = pout[:, cols]
            part[...] += jnp.dot(po, hi, preferred_element_type=F32) + jnp.dot(
                po, lo, preferred_element_type=F32
            )
            return carry

        lax.fori_loop(0, nc // width, columns, 0)
        hi, lo = split2(part[...])
        nt = (((1,), (1,)), ((), ()))
        loc[e] = lax.dot_general(hi, pin[...], nt, preferred_element_type=F32) + lax.dot_general(
            lo, pin[...], nt, preferred_element_type=F32
        )
        rs[me, e] = loc[e, rs_block(me), :]

        def send(k, carry):
            d = (me + k) % nd
            pltpu.make_async_remote_copy(
                src_ref=loc.at[e, rs_block(d), :],
                dst_ref=rs.at[me, e],
                send_sem=rs_send,
                recv_sem=rs_recv,
                device_id=spot(d),
                device_id_type=MESH,
            ).start()
            return carry

        lax.fori_loop(1, nd, send, 0)

    own_sends(0)
    own_sends(1)
    local[0].wait()
    lines = min(256, nc)

    def invert(j, carry):
        rows = pl.ds(pl.multiple_of(j * lines, lines), lines)
        scale[rows, :] = lax.rsqrt(scale[rows, :] + 1e-08)
        return carry

    lax.fori_loop(0, nc // lines, invert, 0)
    local[1].wait()

    def step(s, carry):
        @pl.when(s + 2 < ne)
        def _():
            own_sends(s + 2)

        for d in range(1, nz):
            @pl.when((s - d + 1 >= 0) & (s - d + 1 < ne))
            def _():
                forward(s - d + 1, d)

        @pl.when(s - nz >= 0)
        def _():
            compute(s - nz)

        @pl.when((s - nz + 1 >= 0) & (s - nz + 1 < ne))
        def _():
            load(s - nz + 1)

        return carry

    lax.fori_loop(0, ne + nz, step, 0)

    def sent(e, carry):
        for k in range(1, ncol):
            a_copy(e, k).wait_send()
        for zs in range(nz):
            for k in range(1, nx):
                across(e, zs, k).wait_send()

            @pl.when((zs <= z) & (z < nz - 1))
            def _():
                up(e, zs).wait_send()

            @pl.when((zs >= z) & (z > 0))
            def _():
                down(e, zs).wait_send()

        return carry

    landed = rs.at[pl.ds(0, nd - 1)]
    pltpu.make_async_copy(landed, landed, rs_recv).wait()
    red[...] = lax.fori_loop(1, nd, lambda k, v: v + rs[k], rs[0])
    first = (me * own_rows) % 8 if own_rows < 8 else 0
    squares = jnp.zeros((ne, ki), F32)
    total = jnp.zeros((3 * ne, qbuf.shape[0]), F32)
    for k in range(own_rows):
        row = red[:, first + k, :]
        squares += row * row
        hi = row.astype(BF16).astype(F32)
        mid = (row - hi).astype(BF16).astype(F32)
        lhs = jnp.concatenate([hi, mid, row - hi - mid], axis=0).astype(BF16)
        total += lax.dot_general(
            lhs, qbuf[:, k * ki:(k + 1) * ki], (((1,), (1,)), ((), ())), preferred_element_type=F32
        )
    scores = total[:ne] + total[ne:2 * ne] + total[2 * ne:]
    sq = jnp.broadcast_to(jnp.sum(squares, axis=1, keepdims=True), (ne, 128))
    for p in range(pieces):
        sc_src[p, 0] = scores[:, p * 128:(p + 1) * 128]
        sc_src[p, 1] = sq

    mine = me // stride
    reducer = me % stride == 0

    def to_reducer(p, carry):
        @pl.when(p * stride != me)
        def _():
            pltpu.make_async_remote_copy(
                src_ref=sc_src.at[p],
                dst_ref=sc_buf.at[me],
                send_sem=sc_send,
                recv_sem=sc_recv,
                device_id=spot(p * stride),
                device_id_type=MESH,
            ).start()

        return carry

    lax.fori_loop(0, pieces, to_reducer, 0)

    @pl.when(reducer)
    def _():
        sc_buf[me] = sc_src[mine]
        whole = sc_buf.at[pl.ds(0, nd - 1)]
        pltpu.make_async_copy(whole, whole, sc_recv).wait()
        both = lax.fori_loop(1, nd, lambda k, v: v + sc_buf[k], sc_buf[0])
        fin[mine] = both[0] * lax.rsqrt(both[1] + 1e-06)

        def to_all(k, carry):
            pltpu.make_async_remote_copy(
                src_ref=fin.at[mine],
                dst_ref=fin.at[mine],
                send_sem=fin_send,
                recv_sem=fin_recv,
                device_id=spot((me + k) % nd),
                device_id_type=MESH,
            ).start()
            return carry

        lax.fori_loop(1, nd, to_all, 0)

    lax.fori_loop(0, ne, sent, 0)
    pltpu.make_async_copy(landed, landed, rs_send).wait()

    def finish(count):
        src = sc_src.at[pl.ds(0, count)]
        pltpu.make_async_copy(src, src, sc_send).wait()
        got = fin.at[pl.ds(0, count)]
        pltpu.make_async_copy(got, got, fin_recv).wait()

    @pl.when(reducer)
    def _():
        finish(pieces - 1)
        gone = sc_buf.at[pl.ds(0, nd - 1), 0]
        pltpu.make_async_copy(gone, gone, fin_send).wait()

    @pl.when(jnp.logical_not(reducer))
    def _():
        finish(pieces)

    for p in range(pieces):
        out[:, p * 128:(p + 1) * 128] = fin[p]


def body(nrow, ncol, activations, output_gradients, second_moment, proj_out, proj_in, queries):
    ne, tc, ni = activations.shape
    tr, nc = output_gradients.shape[1:]
    ko, ki = proj_out.shape[0], proj_in.shape[0]
    nq, nf = queries.shape
    nz = 4 if nrow % 4 == 0 else 1
    nd = nrow * ncol
    pieces = nq // 128
    while nd % pieces:
        pieces //= 2
    seq = tr * nrow
    dma = pltpu.SemaphoreType.DMA
    hbm = pl.BlockSpec(memory_space=pl.ANY)
    vmem = pl.BlockSpec(memory_space=pltpu.VMEM)
    return pl.pallas_call(
        functools.partial(kernel, nrow, ncol, nz),
        out_shape=(
            jax.ShapeDtypeStruct((ne, nq), F32),
            jax.ShapeDtypeStruct((ne, seq, nc), BF16),
            jax.ShapeDtypeStruct((ne, seq, ni), BF16),
        ),
        in_specs=[hbm, hbm, hbm, vmem, vmem, hbm],
        out_specs=(vmem, hbm, hbm),
        scratch_shapes=[
            pltpu.VMEM((seq, nc), BF16),
            pltpu.VMEM((seq, ni), BF16),
            pltpu.VMEM((nc, ni), F32),
            pltpu.VMEM((nq, nf), BF16),
            pltpu.VMEM((ko, ni), F32),
            pltpu.VMEM((ne, ko, ki), F32),
            pltpu.VMEM((nd, ne, 8, ki), F32),
            pltpu.VMEM((ne, 8, ki), F32),
            pltpu.VMEM((pieces, 2, ne, 128), F32),
            pltpu.VMEM((nd, 2, ne, 128), F32),
            pltpu.VMEM((pieces, ne, 128), F32),
            dma((2,)),
            dma((nrow + ncol,)),
            dma((ne, nrow)),
            dma((ne, nz)),
            dma((ne, nz)),
            dma((ne, nz, nrow // nz)),
            dma((ne, ncol)),
            dma((ne, ncol)),
            dma, dma, dma, dma, dma, dma,
        ],
        compiler_params=pltpu.CompilerParams(
            collective_id=0, has_side_effects=True, vmem_limit_bytes=58 * 2**20
        ),
    )(activations, output_gradients, second_moment, proj_out, proj_in, queries)[0]


def solution(mesh):
    in_specs = (
        P(None, "col", "row"),
        P(None, "row", "col"),
        P("col", "row"),
        P(None, "col"),
        P(None, "row"),
        P(None, ("row", "col")),
    )
    run = functools.partial(body, mesh.shape["row"], mesh.shape["col"])
    return jax.shard_map(run, mesh=mesh, in_specs=in_specs, out_specs=P(), check_vma=False)
```
